512 devices in a mesh: dp: 2 (over core), ctx: 8 (over z_hi, x), exp: 32 (over z_lo, y).
Axes of the slice: x: 4, y: 8, z: 8 (z_hi: 2, z_lo: 4; z = z_hi * 4 + z_lo), core: 2. Of those that a mesh axis runs over, the one named last changes fastest.
Arguments:
- tokens: bfloat16 [65536, 2048], P(('dp', 'ctx', 'exp')), may hold values from -6 to 6
- cotangent: bfloat16 [65536, 2048], P(('dp', 'ctx', 'exp')), may hold values from -6 to 6
- expert_weights: bfloat16 [32, 768, 6144], P('exp', ('dp', 'ctx')), may hold values from -0.125 to 0.125
- route_ids: int32 [65536, 2], P(('dp', 'ctx', 'exp')), may hold values from 0 to 31, all different within a row; in each aligned block of 128 rows (0 to 127, 128 to 255, ...) at most 12 rows name the same one
- combine: float32 [65536, 2], P(('dp', 'ctx', 'exp')), may hold values from 0.1 to 1
Outputs:
- grad_tokens: bfloat16 [65536, 2048], P(('dp', 'ctx', 'exp'))
- grad_combine: float32 [65536, 2], P(('dp', 'ctx', 'exp'))
The draws below stay inside these ranges and needn't reach their ends.
Inputs may be any that keep to these rules, and one draw needn't show every extreme that they name: `route_ids`: each token names 2 different experts; among the rows of one device no expert is named more than 12 times, a bound that some block reaches.
All inputs are finite; a program needn't handle non-finite values.
Results may differ from the reference program's by a relative error of at most 0.017.
Values may be sent and summed in bfloat16 or wider, within the bound.
A program may use at most 64 MiB of HBM per device.

```python
import math
import jax
import jax.numpy as jnp
import numpy as np
from jax import lax

D = 2048
HID = 768
TOP = 2
TOK_DEV = 128
EXPERTS = 32
CAP = 12
TOKENS = 65536
DEVICES = 512


def block_levels(key, shape, cuts, low, largest):
    factor_of = 1.0
    for dim, shards_of in cuts:
        steps = jax.random.uniform(jax.random.fold_in(jax.random.fold_in(key, 6), dim), (shards_of,), jnp.float32, low / len(cuts), largest / len(cuts))
        factor_of = factor_of * jnp.repeat(jnp.exp(steps), shape[dim] // shards_of).reshape((-1,) + (1,) * (len(shape) - 1 - dim))
    return factor_of


def deal_out(stream_key, own, number, rows, number_of, top, bound, skew):
    order = jax.random.permutation(stream_key, number_of)
    packed, ordinary = portions_of(number_of, rows * top, bound, skew, True), portions_of(number_of, rows * top, bound, skew, False)
    places = jnp.arange(number_of)

    def named(tallies, rotation):
        used = int((tallies > 0).sum())
        fixed = max(1, used // 4)
        passed = fixed + (places - fixed + rotation * (used - fixed)) % max(1, number_of - fixed)
        return jnp.zeros((number_of,), jnp.int32).at[order[jnp.where(places < fixed, places, passed)]].set(jnp.asarray(tallies, jnp.int32))

    tallies = jnp.where(number % 4 == 0, named(packed, number // 4), named(ordinary, number - number // 4 - 1))
    mixed = jax.random.permutation(jax.random.fold_in(own, 3), number_of)
    donor, taker = mixed[0:number_of // 2 * 2:2], mixed[1:number_of // 2 * 2:2]
    slack = jnp.minimum(tallies[donor] - 1, bound - tallies[taker]) // 2
    slack = jnp.where((donor == order[0]) | (taker == order[0]) | (tallies[taker] == 0), 0, jnp.maximum(slack, 0))
    passed = jax.random.randint(jax.random.fold_in(own, 4), (number_of // 2,), 0, 1 << 20) % (slack + 1)
    tallies = tallies.at[donor].add(-passed).at[taker].add(passed)
    items = jnp.searchsorted(jnp.cumsum(tallies), jnp.arange(rows * top), side="right").astype(jnp.int32)
    table = items.reshape(top, rows).T
    table = table[jax.random.permutation(jax.random.fold_in(own, 1), rows)]
    rotation = jax.random.randint(jax.random.fold_in(own, 2), (rows, 1), 0, top)
    return jnp.take_along_axis(table, (jnp.arange(top)[None, :] + rotation) % top, axis=1)


def portions_of(count, total, most, skew, full):
    loads = [(1 << 20) // math.isqrt(rank ** skew) + 1 for rank in range(1, count + 1)]
    largest = most if full else min(most, max(-(-total // count), total * loads[0] // sum(loads)))
    least = 1 if total - largest >= count - 1 else 0
    counts, rest = [largest] + [least] * (count - 1), total - largest - least * (count - 1)
    while rest > 0:
        candidates = [i for i in range(1, count) if counts[i] < largest] or [i for i in range(1, count) if counts[i] < most]
        pool, left = sum([loads[i] for i in candidates]), rest
        for i in candidates:
            addition = min(most - counts[i], max(1, left * loads[i] // pool), rest)
            counts[i] = counts[i] + addition
            rest = rest - addition
    return np.array(counts)


def bell_draw(rng, shape, spread, limit, split=(), kind=jnp.bfloat16):
    drawn = spread * jax.random.normal(rng, shape, jnp.float32)
    if split:
        drawn = drawn * block_levels(rng, shape, split, -0.22, 0.18)
    return jnp.clip(drawn, -limit, limit).astype(kind)


def setup_inputs(seed: int = 0) -> dict:
    seeds = jax.random.split(jax.random.key(seed), 6)
    tokens = bell_draw(seeds[0], (TOKENS, D), 1.0, 6.0, ((0, 512),))
    cotangent = bell_draw(seeds[1], (TOKENS, D), 1.0, 6.0, ((0, 512),))
    expert_weights = bell_draw(seeds[2], (EXPERTS, HID, 3 * D), D ** -0.5, 0.125, ((0, 32), (1, 16)))
    route_ids_keys = jax.random.split(jax.random.fold_in(seeds[3], 1), TOKENS // TOK_DEV)
    route_ids_turns = jax.random.permutation(jax.random.fold_in(seeds[3], 3), TOKENS // TOK_DEV)
    route_ids = jax.vmap(lambda own, number: deal_out(jax.random.fold_in(seeds[3], 2), own, number, TOK_DEV, EXPERTS, TOP, CAP, 2))(route_ids_keys, route_ids_turns).reshape((TOKENS, TOP))
    combine = jnp.clip(0.1 + 0.9 * jax.random.uniform(seeds[4], (TOKENS, TOP), jnp.float32) ** block_levels(seeds[4], (TOKENS, TOP), ((0, 512),), -0.2, 0.2), 0.1, 1.0)
    return dict(tokens=tokens, cotangent=cotangent, expert_weights=expert_weights, route_ids=route_ids, combine=combine)


def silu_parts(gate_pre):
    sigmoid_val = jax.nn.sigmoid(gate_pre)
    return gate_pre * sigmoid_val, sigmoid_val * (1.0 + gate_pre * (1.0 - sigmoid_val))


def expert_rows(x_rows, dy_rows, row_scale, weights):
    model_width = x_rows.shape[1]
    w_gate = weights[:, :model_width]
    w_up = weights[:, model_width:2 * model_width]
    w_down = weights[:, 2 * model_width:]
    gate_pre = jnp.dot(x_rows, w_gate.T, preferred_element_type=jnp.float32)
    up_pre = jnp.dot(x_rows, w_up.T, preferred_element_type=jnp.float32)
    back_proj = jnp.dot(dy_rows, w_down.T, preferred_element_type=jnp.float32)
    active, slopes = silu_parts(gate_pre)
    comb_grad = jnp.sum(back_proj * active * up_pre, axis=1)
    d_hidden = row_scale[:, None] * back_proj
    d_gate = (d_hidden * up_pre * slopes).astype(jnp.bfloat16)
    d_up = (d_hidden * active).astype(jnp.bfloat16)
    slot_grad = jnp.dot(d_gate, w_gate, preferred_element_type=jnp.float32) + jnp.dot(d_up, w_up, preferred_element_type=jnp.float32)
    return slot_grad.astype(jnp.bfloat16), comb_grad


def reference(tokens, cotangent, expert_weights, route_ids, combine):
    flat_ids = route_ids.reshape(-1)
    flat_combine = combine.reshape(-1)
    total_rows = flat_ids.shape[0]
    most_rows = CAP * DEVICES
    row_numbers = jnp.arange(total_rows, dtype=jnp.int32)

    def one_expert(totals, expert):
        grad_acc, comb_acc = totals
        is_match = (flat_ids == expert).astype(jnp.int32)
        ordinal = jnp.cumsum(is_match) - 1
        target = jnp.where(is_match > 0, ordinal, most_rows).astype(jnp.int32)
        picked = jnp.zeros((most_rows,), jnp.int32).at[target].set(row_numbers, mode="drop")
        live_flag = jnp.zeros((most_rows,), jnp.int32).at[target].set(1, mode="drop")
        row_token = picked // TOP
        row_scale = jnp.where(live_flag > 0, flat_combine[picked], jnp.float32(0.0))
        weights = expert_weights[expert]
        slot_grad, comb_grad = expert_rows(tokens[row_token], cotangent[row_token], row_scale, weights)
        live_col = (live_flag > 0)[:, None]
        grad_acc = grad_acc.at[row_token].add(jnp.where(live_col, slot_grad.astype(jnp.float32), jnp.float32(0.0)))
        comb_acc = comb_acc.at[picked].add(jnp.where(live_flag > 0, comb_grad, jnp.float32(0.0)))
        return (grad_acc, comb_acc), None

    start_vals = (jnp.zeros((TOKENS, D), jnp.float32), jnp.zeros((TOKENS * TOP,), jnp.float32))
    (grad_acc, comb_acc), _ = lax.scan(one_expert, start_vals, jnp.arange(EXPERTS, dtype=jnp.int32))
    return grad_acc.astype(jnp.bfloat16), comb_acc.reshape(TOKENS, TOP)
```

```python
import functools

import jax
import jax.numpy as jnp
from jax import lax
from jax.experimental import pallas as pl
from jax.experimental.pallas import tpu as pltpu
from jax.sharding import PartitionSpec as P

MESH = pl.DeviceIdType.MESH
BF16 = jnp.bfloat16
F32 = jnp.float32
ROWS = 128
CAP = 12
BLOCK = 16
BLOCKS = 32
CHUNKS = 4
NX, NY, NZ = 4, 8, 8
D = 2048
SEND = 3 * D // 2
BACK = 3 * D // 4
DY_TAIL = D // 2
G_TAIL = D // 4
UNITS = 768
SHARD = 48
TILE = 256


def place():
    core = lax.axis_index("dp")
    ctx = lax.axis_index("ctx")
    exp = lax.axis_index("exp")
    return core, ctx % NX, exp % NY, (ctx // NX) * 4 + exp // NY


def device(core, x, y, z):
    return (core, (z // 4) * NX + x, (z % 4) * NY + y)


def partner(me, step_y, step_z):
    core, x, y, z = me
    far = jnp.where(step_z == 2, ((z // 2) % 2 + core) % 2, jnp.where(step_z == 3, 1, 0))
    return device(core, x, (y + step_y) % NY, (z + step_z + 4 * far) % NZ)


def iota(shape, dim):
    return lax.broadcasted_iota(jnp.int32, shape, dim)


def nt(a, b):
    return lax.dot_general(a, b, (((1,), (1,)), ((), ())), preferred_element_type=F32)


def nn(a, b):
    return jnp.dot(a, b, preferred_element_type=F32)


def one(cond):
    return jnp.where(cond, 1.0, 0.0).astype(BF16)


def kernel(
    tok, cot, w_ref, rid, cmb, out, gcomb,
    wb, xs, xr, gs, gr, tail, acc, home, cs, cr, vx, vxt,
    local_sem, w_send, w_recv, x_send, x_recv, g_send, g_recv, c_send, c_recv,
):
    me = place()
    core, x, y, z = me
    barrier = pltpu.get_barrier_semaphore()

    def greet(k, carry):
        pl.semaphore_signal(
            barrier, inc=1, device_id=partner(me, k % NY, k // NY), device_id_type=MESH
        )
        return carry

    lax.fori_loop(1, BLOCKS, greet, 0)
    z_far = device(core, x, y, (z + 4) % NZ)
    x_up = device(core, (x + 1) % NX, y, z)
    x_down = device(core, (x + 3) % NX, y, z)
    twin = device(1 - core, x, y, z)
    for other in (z_far, x_up, x_down, twin):
        pl.semaphore_signal(barrier, inc=1, device_id=other, device_id_type=MESH)

    def shard(half, side, step):
        return wb.at[pl.ds((half * 8 + side * 4 + step) * SHARD, SHARD), :]

    own_copy = pltpu.make_async_copy(w_ref, shard(0, 0, 0), local_sem.at[0])
    own_copy.start()

    ids = rid[...]
    rel = ((ids // NY - z % 4 + 4) % 4) * NY + (ids % NY - y + NY) % NY
    first, second = rel[:, 0:1], rel[:, 1:2]
    lane = iota((ROWS, ROWS), 1)
    sub = iota((ROWS, ROWS), 0)
    named = (first == lane) | (second == lane)
    ordinal = nn(one(lane < sub), one(named))
    val = jnp.where(named, ordinal, -1.0).astype(BF16)
    slots = BLOCKS * BLOCK
    spread = one(iota((slots, ROWS), 0) // BLOCK == iota((slots, ROWS), 1))
    vxt[...] = nt(spread, val)
    vx[...] = nt(val, spread)

    pl.semaphore_wait(barrier, BLOCKS - 1 + 4)

    def send_w(n, src, dst, target):
        copy = pltpu.make_async_remote_copy(
            src_ref=src, dst_ref=dst, send_sem=w_send.at[n], recv_sem=w_recv.at[n],
            device_id=target, device_id_type=MESH,
        )
        copy.start()
        return copy

    z_copy = send_w(0, w_ref, shard(1, 0, 0), z_far)
    up0 = send_w(1, w_ref, shard(0, 0, 1), x_up)
    down0 = send_w(2, w_ref, shard(0, 0, 3), x_down)
    twin00 = send_w(3, w_ref, shard(0, 1, 0), twin)

    def x_copy(k):
        rows = pl.ds(pl.multiple_of(k * BLOCK, BLOCK), BLOCK)
        return pltpu.make_async_remote_copy(
            src_ref=xs.at[rows, :], dst_ref=xr.at[rows, :],
            send_sem=x_send.at[k], recv_sem=x_recv.at[k],
            device_id=partner(me, k % NY, k // NY), device_id_type=MESH,
        )

    def g_copy(k):
        rows = pl.ds(pl.multiple_of(k * BLOCK, BLOCK), BLOCK)
        return pltpu.make_async_remote_copy(
            src_ref=gs.at[rows, :], dst_ref=gr.at[rows, :],
            send_sem=g_send.at[k], recv_sem=g_recv.at[k],
            device_id=partner(me, (NY - k % NY) % NY, (4 - k // NY) % 4), device_id_type=MESH,
        )

    def c_copy(k):
        return pltpu.make_async_remote_copy(
            src_ref=cs.at[k // NY], dst_ref=cr.at[k],
            send_sem=c_send.at[k], recv_sem=c_recv.at[k],
            device_id=partner(me, (NY - k % NY) % NY, (4 - k // NY) % 4), device_id_type=MESH,
        )

    def each(chunk, act):
        def step(i, carry):
            act(chunk * 8 + i)
            return carry
        lax.fori_loop(jnp.where(chunk == 0, 1, 0), 8, step, 0)

    def dispatch(chunk, carry):
        rows = pl.ds(pl.multiple_of(chunk * ROWS, ROWS), ROWS)
        v = vxt[rows, :].astype(jnp.int32)
        row = sub % BLOCK
        put = one((v == row) & (row < CAP))
        ends = cot[:, DY_TAIL:]
        pieces = (tok[:, :DY_TAIL], tok[:, DY_TAIL:], cot[:, :DY_TAIL])
        for j, piece in enumerate(pieces):
            put_end = one((v == 3 * (row - CAP) + j) & (row >= CAP))
            got = nn(put, piece) + nn(put_end, ends)
            xs[rows, j * DY_TAIL : (j + 1) * DY_TAIL] = got.astype(BF16)
        each(chunk, lambda k: x_copy(k).start())
        return carry

    lax.fori_loop(0, CHUNKS, dispatch, 0)
    xr[0:BLOCK, :] = xs[0:BLOCK, :]

    started = [z_copy, up0, down0, twin00]

    def pass_on(n, half, step, target, to_step, side=0):
        started.append(send_w(n, shard(half, 0, step), shard(half, side, to_step), target))

    up0.wait_recv()
    pass_on(4, 0, 1, x_up, 2)
    pass_on(5, 0, 1, twin, 1, side=1)
    down0.wait_recv()
    pass_on(6, 0, 3, twin, 3, side=1)
    z_copy.wait_recv()
    pass_on(7, 1, 0, x_up, 1)
    pass_on(8, 1, 0, x_down, 3)
    pass_on(9, 1, 0, twin, 0, side=1)
    started[4].wait_recv()
    pass_on(10, 0, 2, twin, 2, side=1)
    started[8].wait_recv()
    pass_on(11, 1, 3, x_down, 2)
    pass_on(12, 1, 3, twin, 3, side=1)
    started[7].wait_recv()
    pass_on(13, 1, 1, twin, 1, side=1)
    started[11].wait_recv()
    pass_on(14, 1, 2, twin, 2, side=1)
    for n in (3, 5, 6, 9, 10, 12, 13, 14):
        started[n].wait_recv()
    own_copy.wait()

    row = sub % BLOCK
    col = lane % BLOCK
    same = sub // BLOCK == lane // BLOCK

    def work(chunk, carry):
        each(chunk, lambda k: x_copy(k).wait_recv())
        rows = pl.ds(pl.multiple_of(chunk * ROWS, ROWS), ROWS)
        end = jnp.zeros((ROWS, DY_TAIL), F32)
        for j in range(3):
            take = one(same & (col >= CAP) & (row == 3 * (col - CAP) + j))
            end = end + nn(take, xr[rows, j * DY_TAIL : (j + 1) * DY_TAIL])
        tail[...] = end.astype(BF16)

        def units(t, total):
            us = pl.ds(pl.multiple_of(t * TILE, TILE), TILE)
            xv = xr[rows, 0:D]
            gate = nt(xv, wb[us, 0:D])
            up = nt(xv, wb[us, D : 2 * D])
            back = nt(xr[rows, D : D + DY_TAIL], wb[us, 2 * D : 2 * D + DY_TAIL])
            back = back + nt(tail[...], wb[us, 2 * D + DY_TAIL : 3 * D])
            sig = jax.nn.sigmoid(gate)
            act = gate * sig
            d_up = back * act
            d_gate = back * up * (sig * (1.0 + gate * (1.0 - sig)))
            got = nn(d_gate.astype(BF16), wb[us, 0:D]) + nn(d_up.astype(BF16), wb[us, D : 2 * D])

            @pl.when(t == 0)
            def _():
                acc[...] = got

            @pl.when(t > 0)
            def _():
                acc[...] += got

            return total + jnp.sum(d_up * up, axis=1, keepdims=True)

        total = lax.fori_loop(0, UNITS // TILE, units, jnp.zeros((ROWS, 1), F32))
        cs[chunk] = jnp.transpose(jnp.broadcast_to(total, (ROWS, ROWS)))[0:1, :]
        ends = acc[:, BACK:D].astype(BF16)
        for j in range(3):
            cols = slice(j * G_TAIL, (j + 1) * G_TAIL)
            take = one(same & (row >= CAP) & (col == 3 * (row - CAP) + j))
            moved = nn(take, ends)
            keep = iota((ROWS, G_TAIL), 0) % BLOCK < CAP
            gs[rows, cols] = jnp.where(keep, acc[:, cols], moved).astype(BF16)

        def give(k):
            g_copy(k).start()
            c_copy(k).start()

        each(chunk, give)
        return carry

    lax.fori_loop(0, CHUNKS, work, 0)
    gr[0:BLOCK, :] = gs[0:BLOCK, :]
    cr[0] = cs[0]

    c0, c1 = cmb[:, 0:1], cmb[:, 1:2]

    def gather(chunk, carry):
        each(chunk, lambda k: (g_copy(k).wait_recv(), c_copy(k).wait_recv()))
        rows = pl.ds(pl.multiple_of(chunk * ROWS, ROWS), ROWS)
        v = vx[:, rows].astype(jnp.int32)
        block = chunk * 8 + lane // BLOCK
        at0, at1 = first == block, second == block
        hit = (v == col) & (col < CAP)
        hit0, hit1 = hit & at0, hit & at1
        end = jnp.zeros((ROWS, G_TAIL), F32)
        for j in range(3):
            cols = slice(j * G_TAIL, (j + 1) * G_TAIL)
            part = gr[rows, cols]
            got = c0 * nn(one(hit0), part) + c1 * nn(one(hit1), part)
            hit_end = (v == 3 * (col - CAP) + j) & (col >= CAP)
            end = end + c0 * nn(one(hit_end & at0), part) + c1 * nn(one(hit_end & at1), part)

            @pl.when(chunk == 0)
            def _():
                home[:, cols] = got

            @pl.when(chunk > 0)
            def _():
                home[:, cols] += got

        @pl.when(chunk == 0)
        def _():
            home[:, BACK:D] = end

        @pl.when(chunk > 0)
        def _():
            home[:, BACK:D] += end

        line = jnp.zeros((1, ROWS), F32)
        for i in range(8):
            line = jnp.where(iota((1, ROWS), 1) // BLOCK == i, cr[chunk * 8 + i], line)
        g0, g1 = carry
        g0 = g0 + jnp.sum(jnp.where(hit0, line, 0.0), axis=1, keepdims=True)
        g1 = g1 + jnp.sum(jnp.where(hit1, line, 0.0), axis=1, keepdims=True)
        return g0, g1

    zero = jnp.zeros((ROWS, 1), F32)
    g0, g1 = lax.fori_loop(0, CHUNKS, gather, (zero, zero))
    out[...] = home[...].astype(BF16)
    gcomb[...] = jnp.where(iota((ROWS, 2), 1) == 0, g0, g1)

    def finish(k, carry):
        x_copy(k).wait_send()
        g_copy(k).wait_send()
        c_copy(k).wait_send()
        return carry

    lax.fori_loop(1, BLOCKS, finish, 0)
    for copy in started:
        copy.wait_send()


def body(tokens, cotangent, expert_weights, route_ids, combine):
    vmem = pl.BlockSpec(memory_space=pltpu.VMEM)
    slots = BLOCKS * BLOCK
    dma = pltpu.SemaphoreType.DMA
    return pl.pallas_call(
        kernel,
        out_shape=(
            jax.ShapeDtypeStruct((ROWS, D), BF16),
            jax.ShapeDtypeStruct((ROWS, 2), F32),
        ),
        in_specs=[vmem, vmem, pl.BlockSpec(memory_space=pl.ANY), vmem, vmem],
        out_specs=(vmem, vmem),
        scratch_shapes=[
            pltpu.VMEM((UNITS, 3 * D), BF16),
            pltpu.VMEM((slots, SEND), BF16),
            pltpu.VMEM((slots, SEND), BF16),
            pltpu.VMEM((slots, BACK), BF16),
            pltpu.VMEM((slots, BACK), BF16),
            pltpu.VMEM((ROWS, DY_TAIL), BF16),
            pltpu.VMEM((ROWS, D), F32),
            pltpu.VMEM((ROWS, D), F32),
            pltpu.VMEM((CHUNKS, 1, ROWS), F32),
            pltpu.VMEM((BLOCKS, 1, ROWS), F32),
            pltpu.VMEM((ROWS, slots), F32),
            pltpu.VMEM((slots, ROWS), F32),
            dma((1,)),
            dma((15,)), dma((15,)),
            dma((BLOCKS,)), dma((BLOCKS,)),
            dma((BLOCKS,)), dma((BLOCKS,)),
            dma((BLOCKS,)), dma((BLOCKS,)),
        ],
        compiler_params=pltpu.CompilerParams(
            collective_id=0, has_side_effects=True, vmem_limit_bytes=48 << 20
        ),
        cost_estimate=pl.CostEstimate(flops=8 << 30, bytes_accessed=4 << 20, transcendentals=1 << 20),
    )(tokens, cotangent, expert_weights[0], route_ids, combine)


def solution(mesh):
    rows = P(("dp", "ctx", "exp"), None)
    return jax.shard_map(
        body,
        mesh=mesh,
        in_specs=(rows, rows, P("exp", ("dp", "ctx"), None), rows, rows),
        out_specs=(rows, rows),
        check_vma=False,
    )
```

```python
import functools

import jax
import jax.numpy as jnp
from jax import lax
from jax.experimental import pallas as pl
from jax.experimental.pallas import tpu as pltpu
from jax.sharding import PartitionSpec as P

MESH = pl.DeviceIdType.MESH
BF16 = jnp.bfloat16
F32 = jnp.float32
ROWS = 128
CAP = 12
BLOCK = 16
BLOCKS = 32
GROUPS = 4
WIDE = 256
NX, NY, NZ = 4, 8, 8
D = 2048
SEND = 3 * D // 2
BACK = 3 * D // 4
DY_TAIL = D // 2
G_TAIL = D // 4
UNITS = 768
SHARD = 48
PIECE = 16
W_COPIES = 31
TILE = 256


def place():
    core = lax.axis_index("dp")
    ctx = lax.axis_index("ctx")
    exp = lax.axis_index("exp")
    return core, ctx % NX, exp % NY, (ctx // NX) * 4 + exp // NY


def device(core, x, y, z):
    return (core, (z // 4) * NX + x, (z % 4) * NY + y)


def partner(me, step_y, step_z):
    core, x, y, z = me
    far = jnp.where(step_z == 2, ((z // 2) % 2 + core) % 2, jnp.where(step_z == 3, 1, 0))
    return device(core, x, (y + step_y) % NY, (z + step_z + 4 * far) % NZ)


def step_of(group):
    return jnp.where(group < 2, group, 5 - group)


def iota(shape, dim):
    return lax.broadcasted_iota(jnp.int32, shape, dim)


def nt(a, b):
    return lax.dot_general(a, b, (((1,), (1,)), ((), ())), preferred_element_type=F32)


def nn(a, b):
    return jnp.dot(a, b, preferred_element_type=F32)


def one(cond):
    return jnp.where(cond, 1.0, 0.0).astype(BF16)


def kernel(
    tok_hbm, cot_hbm, w_ref, rid_hbm, cmb_hbm, out, gcomb,
    tok, cot, rid, cmb, wb, xs, xr, gs, gr, tail, ends, dgs, dus, home, cs, cr, vx, vxt,
    local_sem, w_send, w_recv, x_send, x_recv, g_send, g_recv, c_send, c_recv,
):
    me = place()
    core, x, y, z = me
    barrier = pltpu.get_barrier_semaphore()

    def greet(k, carry):
        pl.semaphore_signal(
            barrier, inc=1, device_id=partner(me, k % NY, step_of(k // NY)), device_id_type=MESH
        )
        return carry

    lax.fori_loop(1, BLOCKS, greet, 0)
    z_far = device(core, x, y, (z + 4) % NZ)
    x_up = device(core, (x + 1) % NX, y, z)
    x_down = device(core, (x + 3) % NX, y, z)
    twin = device(1 - core, x, y, z)
    for other in (z_far, x_up, x_down, twin):
        pl.semaphore_signal(barrier, inc=1, device_id=other, device_id_type=MESH)

    def shard(half, side, step, piece=None):
        at = (half * 8 + side * 4 + step) * SHARD
        if piece is None:
            return wb.at[pl.ds(at, SHARD), :]
        return wb.at[pl.ds(at + piece * PIECE, PIECE), :]

    loads = []
    for n, (src, dst) in enumerate(
        ((rid_hbm, rid), (tok_hbm, tok), (cot_hbm, cot), (cmb_hbm, cmb), (w_ref, shard(0, 0, 0)))
    ):
        load = pltpu.make_async_copy(src, dst, local_sem.at[n])
        load.start()
        loads.append(load)
    loads[0].wait()

    ids = rid[...]
    step_z = (ids // NY - z % 4 + 4) % 4
    rel = (step_of(step_z) * NY + (ids % NY - y + NY) % NY).astype(F32)

    def column(line):
        return jnp.transpose(jnp.broadcast_to(line, (ROWS, ROWS)))

    first = column(rel[0:1, :]).astype(jnp.int32)
    second = column(rel[1:2, :]).astype(jnp.int32)
    lane = iota((ROWS, ROWS), 1)
    sub = iota((ROWS, ROWS), 0)
    named = (first == lane) | (second == lane)
    ordinal = nn(one(lane < sub), one(named))
    val = jnp.where(named, ordinal, -1.0).astype(BF16)
    slots = BLOCKS * BLOCK
    spread = one(iota((slots, ROWS), 0) // BLOCK == iota((slots, ROWS), 1))
    vxt[...] = nt(spread, val)
    vx[...] = nt(val, spread)

    pl.semaphore_wait(barrier, BLOCKS - 1 + 4)

    started = []

    def send_w(src, dst, target):
        n = len(started)
        copy = pltpu.make_async_remote_copy(
            src_ref=src, dst_ref=dst, send_sem=w_send.at[n], recv_sem=w_recv.at[n],
            device_id=target, device_id_type=MESH,
        )
        copy.start()
        started.append(copy)
        return copy

    pieces = range(SHARD // PIECE)
    z_in = [
        send_w(w_ref.at[pl.ds(p * PIECE, PIECE), :], shard(1, 0, 0, p), z_far) for p in pieces
    ]
    up0 = send_w(w_ref, shard(0, 0, 1), x_up)
    down0 = send_w(w_ref, shard(0, 0, 3), x_down)
    twins = [send_w(w_ref, shard(0, 1, 0), twin)]

    def x_copy(k):
        rows = pl.ds(pl.multiple_of(k * BLOCK, BLOCK), BLOCK)
        return pltpu.make_async_remote_copy(
            src_ref=xs.at[rows, :], dst_ref=xr.at[rows, :],
            send_sem=x_send.at[k], recv_sem=x_recv.at[k],
            device_id=partner(me, k % NY, step_of(k // NY)), device_id_type=MESH,
        )

    def source(k):
        return partner(me, (NY - k % NY) % NY, (4 - step_of(k // NY)) % 4)

    def g_copy(k):
        rows = pl.ds(pl.multiple_of(k * BLOCK, BLOCK), BLOCK)
        return pltpu.make_async_remote_copy(
            src_ref=gs.at[rows, :], dst_ref=gr.at[rows, :],
            send_sem=g_send.at[k], recv_sem=g_recv.at[k],
            device_id=source(k), device_id_type=MESH,
        )

    def c_copy(k):
        return pltpu.make_async_remote_copy(
            src_ref=cs.at[k // NY], dst_ref=cr.at[k],
            send_sem=c_send.at[k], recv_sem=c_recv.at[k],
            device_id=source(k), device_id_type=MESH,
        )

    def loop(low, high, act):
        def step(i, carry):
            act(i)
            return carry
        lax.fori_loop(low, high, step, 0)

    loads[1].wait()
    loads[2].wait()

    def dispatch(group):
        rows = pl.ds(pl.multiple_of(group * ROWS, ROWS), ROWS)
        v = vxt[rows, :].astype(jnp.int32)
        row = sub % BLOCK
        put = one((v == row) & (row < CAP))
        parts = (tok[:, :DY_TAIL], tok[:, DY_TAIL:], cot[:, :DY_TAIL])
        for j, part in enumerate(parts):
            put_end = one((v == 3 * (row - CAP) + j) & (row >= CAP))
            got = nn(put, part) + nn(put_end, cot[:, DY_TAIL:])
            xs[rows, j * DY_TAIL : (j + 1) * DY_TAIL] = got.astype(BF16)

    dispatch(0)
    loop(1, 8, lambda k: x_copy(k).start())
    loop(1, 3, dispatch)

    def two(i):
        x_copy(8 + i).start()
        x_copy(16 + (i + 4) % 8).start()

    loop(0, 8, two)
    dispatch(3)
    loop(24, 32, lambda k: x_copy(k).start())
    xr[0:BLOCK, :] = xs[0:BLOCK, :]

    up, down, across = [], [], []

    def to_twin(half, step, piece=None):
        twins.append(send_w(shard(half, 0, step, piece), shard(half, 1, step, piece), twin))

    def from_z(p):
        z_in[p].wait_recv()
        up.append(send_w(shard(1, 0, 0, p), shard(1, 0, 1, p), x_up))
        down.append(send_w(shard(1, 0, 0, p), shard(1, 0, 3, p), x_down))
        to_twin(1, 0, p)

    def from_x(p):
        down[p].wait_recv()
        across.append(send_w(shard(1, 0, 3, p), shard(1, 0, 2, p), x_down))
        to_twin(1, 3, p)
        up[p].wait_recv()
        to_twin(1, 1, p)

    def from_across(p):
        across[p].wait_recv()
        to_twin(1, 2, p)

    up0.wait_recv()
    across0 = send_w(shard(0, 0, 1), shard(0, 0, 2), x_up)
    to_twin(0, 1)
    down0.wait_recv()
    to_twin(0, 3)
    from_z(0)
    across0.wait_recv()
    to_twin(0, 2)
    from_z(1)
    from_x(0)
    from_z(2)
    from_x(1)
    from_across(0)
    from_x(2)
    from_across(1)
    from_across(2)
    for copy in twins:
        copy.wait_recv()
    loads[4].wait()

    sub2 = iota((WIDE, WIDE), 0)
    lane2 = iota((WIDE, WIDE), 1)
    row2 = sub2 % BLOCK
    col2 = lane2 % BLOCK
    same2 = sub2 // BLOCK == lane2 // BLOCK

    def work(chunk):
        loop(jnp.where(chunk == 0, 1, 16), 16 + 16 * chunk, lambda k: x_copy(k).wait_recv())
        rows = pl.ds(pl.multiple_of(chunk * WIDE, WIDE), WIDE)
        end = jnp.zeros((WIDE, DY_TAIL), F32)
        for j in range(3):
            take = one(same2 & (col2 >= CAP) & (row2 == 3 * (col2 - CAP) + j))
            end = end + nn(take, xr[rows, j * DY_TAIL : (j + 1) * DY_TAIL])
        tail[...] = end.astype(BF16)

        def units(t, total):
            us = pl.ds(pl.multiple_of(t * TILE, TILE), TILE)
            xv = xr[rows, 0:D]
            gate = nt(xv, wb[us, 0:D])
            up_pre = nt(xv, wb[us, D : 2 * D])
            back = nt(xr[rows, D : D + DY_TAIL], wb[us, 2 * D : 2 * D + DY_TAIL])
            back = back + nt(tail[...], wb[us, 2 * D + DY_TAIL : 3 * D])
            sig = jax.nn.sigmoid(gate)
            act = gate * sig
            d_up = back * act
            d_gate = back * up_pre * (sig * (1.0 + gate * (1.0 - sig)))
            dgs[:, us] = d_gate.astype(BF16)
            dus[:, us] = d_up.astype(BF16)
            return total + jnp.sum(d_up * up_pre, axis=1, keepdims=True)

        total = lax.fori_loop(0, UNITS // TILE, units, jnp.zeros((WIDE, 1), F32))
        for h in range(2):
            part = jnp.broadcast_to(total[h * ROWS : (h + 1) * ROWS, :], (ROWS, ROWS))
            cs[chunk * 2 + h] = jnp.transpose(part)[0:1, :]

        def grad(low):
            high = low + G_TAIL
            return nn(dgs[...], wb[:, low:high]) + nn(dus[...], wb[:, D + low : D + high])

        ends[...] = grad(BACK).astype(BF16)
        for j in range(3):
            take = one(same2 & (row2 >= CAP) & (col2 == 3 * (row2 - CAP) + j))
            moved = nn(take, ends[...])
            keep = iota((WIDE, G_TAIL), 0) % BLOCK < CAP
            both = jnp.where(keep, grad(j * G_TAIL), moved).astype(BF16)
            gs[rows, j * G_TAIL : (j + 1) * G_TAIL] = both

        def give(i):
            for k in (chunk * 16 + i, chunk * 16 + 8 + (i + 4) % 8):
                @pl.when(k > 0)
                def _():
                    g_copy(k).start()
                    c_copy(k).start()

        loop(0, 8, give)

    loop(0, 2, work)
    gr[0:BLOCK, :] = gs[0:BLOCK, :]
    cr[0] = cs[0]

    loads[3].wait()
    c0, c1 = column(cmb[0:1, :])[:, 0:1], column(cmb[1:2, :])[:, 0:1]
    col = lane % BLOCK

    def gather(group, carry):
        def arrived(k):
            g_copy(k).wait_recv()
            c_copy(k).wait_recv()

        loop(jnp.where(group == 0, 1, group * 8), group * 8 + 8, arrived)
        rows = pl.ds(pl.multiple_of(group * ROWS, ROWS), ROWS)
        v = vx[:, rows].astype(jnp.int32)
        block = group * 8 + lane // BLOCK
        at0, at1 = first == block, second == block
        hit = (v == col) & (col < CAP)
        hit0, hit1 = hit & at0, hit & at1
        end = jnp.zeros((ROWS, G_TAIL), F32)
        for j in range(3):
            cols = slice(j * G_TAIL, (j + 1) * G_TAIL)
            part = gr[rows, cols]
            got = c0 * nn(one(hit0), part) + c1 * nn(one(hit1), part)
            hit_end = (v == 3 * (col - CAP) + j) & (col >= CAP)
            end = end + c0 * nn(one(hit_end & at0), part) + c1 * nn(one(hit_end & at1), part)

            @pl.when(group == 0)
            def _():
                home[:, cols] = got

            @pl.when(group > 0)
            def _():
                home[:, cols] += got

        @pl.when(group == 0)
        def _():
            home[:, BACK:D] = end

        @pl.when(group > 0)
        def _():
            home[:, BACK:D] += end

        line = jnp.zeros((1, ROWS), F32)
        for i in range(8):
            line = jnp.where(iota((1, ROWS), 1) // BLOCK == i, cr[group * 8 + i], line)
        g0, g1 = carry
        g0 = g0 + jnp.sum(jnp.where(hit0, line, 0.0), axis=1, keepdims=True)
        g1 = g1 + jnp.sum(jnp.where(hit1, line, 0.0), axis=1, keepdims=True)
        return g0, g1

    zero = jnp.zeros((ROWS, 1), F32)
    g0, g1 = lax.fori_loop(0, GROUPS, gather, (zero, zero))
    out[...] = home[...].astype(BF16)
    gcomb[0:1, :] = jnp.transpose(jnp.broadcast_to(g0, (ROWS, ROWS)))[0:1, :]
    gcomb[1:2, :] = jnp.transpose(jnp.broadcast_to(g1, (ROWS, ROWS)))[0:1, :]

    def finish(k):
        x_copy(k).wait_send()
        g_copy(k).wait_send()
        c_copy(k).wait_send()

    loop(1, BLOCKS, finish)
    for copy in started:
        copy.wait_send()


def body(tokens, cotangent, expert_weights, route_ids, combine):
    vmem = pl.BlockSpec(memory_space=pltpu.VMEM)
    hbm = pl.BlockSpec(memory_space=pltpu.HBM)
    slots = BLOCKS * BLOCK
    dma = pltpu.SemaphoreType.DMA
    grad_tokens, grad_combine = pl.pallas_call(
        kernel,
        out_shape=(
            jax.ShapeDtypeStruct((ROWS, D), BF16),
            jax.ShapeDtypeStruct((2, ROWS), F32),
        ),
        in_specs=[hbm] * 5,
        out_specs=(vmem, vmem),
        scratch_shapes=[
            pltpu.VMEM((ROWS, D), BF16),
            pltpu.VMEM((ROWS, D), BF16),
            pltpu.VMEM((2, ROWS), jnp.int32),
            pltpu.VMEM((2, ROWS), F32),
            pltpu.VMEM((UNITS, 3 * D), BF16),
            pltpu.VMEM((slots, SEND), BF16),
            pltpu.VMEM((slots, SEND), BF16),
            pltpu.VMEM((slots, BACK), BF16),
            pltpu.VMEM((slots, BACK), BF16),
            pltpu.VMEM((WIDE, DY_TAIL), BF16),
            pltpu.VMEM((WIDE, G_TAIL), BF16),
            pltpu.VMEM((WIDE, UNITS), BF16),
            pltpu.VMEM((WIDE, UNITS), BF16),
            pltpu.VMEM((ROWS, D), F32),
            pltpu.VMEM((GROUPS, 1, ROWS), F32),
            pltpu.VMEM((BLOCKS, 1, ROWS), F32),
            pltpu.VMEM((ROWS, slots), F32),
            pltpu.VMEM((slots, ROWS), F32),
            dma((5,)),
            dma((W_COPIES,)), dma((W_COPIES,)),
            dma((BLOCKS,)), dma((BLOCKS,)),
            dma((BLOCKS,)), dma((BLOCKS,)),
            dma((BLOCKS,)), dma((BLOCKS,)),
        ],
        compiler_params=pltpu.CompilerParams(
            collective_id=0, has_side_effects=True, vmem_limit_bytes=56 << 20
        ),
        cost_estimate=pl.CostEstimate(flops=8 << 30, bytes_accessed=4 << 20, transcendentals=1 << 20),
    )(tokens, cotangent, expert_weights[0], route_ids.T, combine.T)
    return grad_tokens, grad_combine.T


def solution(mesh):
    rows = P(("dp", "ctx", "exp"), None)
    return jax.shard_map(
        body,
        mesh=mesh,
        in_specs=(rows, rows, P("exp", ("dp", "ctx"), None), rows, rows),
        out_specs=(rows, rows),
        check_vma=False,
    )
```

```python
import functools

import jax
import jax.numpy as jnp
from jax import lax
from jax.experimental import pallas as pl
from jax.experimental.pallas import tpu as pltpu
from jax.sharding import PartitionSpec as P

MESH = pl.DeviceIdType.MESH
BF16 = jnp.bfloat16
F32 = jnp.float32
ROWS = 128
CAP = 12
BLOCK = 16
BLOCKS = 32
GROUPS = 4
WIDE = 256
NX, NY, NZ = 4, 8, 8
D = 2048
SEND = 3 * D // 2
BACK = 3 * D // 4
DY_TAIL = D // 2
G_TAIL = D // 4
UNITS = 768
SHARD = 48
PIECE = 16
W_COPIES = 31
TILE = 256


def place():
    core = lax.axis_index("dp")
    ctx = lax.axis_index("ctx")
    exp = lax.axis_index("exp")
    return core, ctx % NX, exp % NY, (ctx // NX) * 4 + exp // NY


def device(core, x, y, z):
    return (core, (z // 4) * NX + x, (z % 4) * NY + y)


def partner(me, step_y, step_z):
    core, x, y, z = me
    far = jnp.where(step_z == 2, ((z // 2) % 2 + core) % 2, jnp.where(step_z == 3, 1, 0))
    return device(core, x, (y + step_y) % NY, (z + step_z + 4 * far) % NZ)


def table(index, values):
    found = jnp.full_like(index, values[0])
    for i, value in enumerate(values[1:]):
        found = jnp.where(index == i + 1, value, found)
    return found


def steps(k):
    return table(k // 4, (0, 4, 3, 5, 1, 7, 2, 6)), k % 4


def iota(shape, dim):
    return lax.broadcasted_iota(jnp.int32, shape, dim)


def nt(a, b):
    return lax.dot_general(a, b, (((1,), (1,)), ((), ())), preferred_element_type=F32)


def nn(a, b):
    return jnp.dot(a, b, preferred_element_type=F32)


def one(cond):
    return jnp.where(cond, 1.0, 0.0).astype(BF16)


def kernel(
    tok_hbm, cot_hbm, w_ref, rid_hbm, cmb_hbm, out, gcomb,
    tok, cot, rid, cmb, wb, xs, xr, gs, gr, tail, ends, dgs, dus, home, cs, cr, vx, vxt,
    local_sem, w_send, w_recv, x_send, x_recv, g_send, g_recv, c_send, c_recv,
):
    me = place()
    core, x, y, z = me
    barrier = pltpu.get_barrier_semaphore()

    def greet(k, carry):
        pl.semaphore_signal(
            barrier, inc=1, device_id=partner(me, *steps(k)), device_id_type=MESH
        )
        return carry

    lax.fori_loop(1, BLOCKS, greet, 0)
    z_far = device(core, x, y, (z + 4) % NZ)
    x_up = device(core, (x + 1) % NX, y, z)
    x_down = device(core, (x + 3) % NX, y, z)
    twin = device(1 - core, x, y, z)
    for other in (z_far, x_up, x_down, twin):
        pl.semaphore_signal(barrier, inc=1, device_id=other, device_id_type=MESH)

    def shard(half, side, step, piece=None):
        at = (half * 8 + side * 4 + step) * SHARD
        if piece is None:
            return wb.at[pl.ds(at, SHARD), :]
        return wb.at[pl.ds(at + piece * PIECE, PIECE), :]

    loads = []
    for n, (src, dst) in enumerate(
        ((rid_hbm, rid), (tok_hbm, tok), (cot_hbm, cot), (cmb_hbm, cmb), (w_ref, shard(0, 0, 0)))
    ):
        load = pltpu.make_async_copy(src, dst, local_sem.at[n])
        load.start()
        loads.append(load)
    loads[0].wait()

    ids = rid[...]
    step_z = (ids // NY - z % 4 + 4) % 4
    step_y = (ids % NY - y + NY) % NY
    rel = (table(step_y, (0, 4, 6, 2, 1, 3, 7, 5)) * 4 + step_z).astype(F32)

    def column(line):
        return jnp.transpose(jnp.broadcast_to(line, (ROWS, ROWS)))

    first = column(rel[0:1, :]).astype(jnp.int32)
    second = column(rel[1:2, :]).astype(jnp.int32)
    lane = iota((ROWS, ROWS), 1)
    sub = iota((ROWS, ROWS), 0)
    named = (first == lane) | (second == lane)
    ordinal = nn(one(lane < sub), one(named))
    val = jnp.where(named, ordinal, -1.0).astype(BF16)
    slots = BLOCKS * BLOCK
    spread = one(iota((slots, ROWS), 0) // BLOCK == iota((slots, ROWS), 1))
    vxt[...] = nt(spread, val)
    vx[...] = nt(val, spread)

    pl.semaphore_wait(barrier, BLOCKS - 1 + 4)

    started = []

    def send_w(src, dst, target):
        n = len(started)
        copy = pltpu.make_async_remote_copy(
            src_ref=src, dst_ref=dst, send_sem=w_send.at[n], recv_sem=w_recv.at[n],
            device_id=target, device_id_type=MESH,
        )
        copy.start()
        started.append(copy)
        return copy

    pieces = range(SHARD // PIECE)
    z_in = [
        send_w(w_ref.at[pl.ds(p * PIECE, PIECE), :], shard(1, 0, 0, p), z_far) for p in pieces
    ]
    up0 = send_w(w_ref, shard(0, 0, 1), x_up)
    down0 = send_w(w_ref, shard(0, 0, 3), x_down)
    twins = [send_w(w_ref, shard(0, 1, 0), twin)]

    def x_copy(k):
        rows = pl.ds(pl.multiple_of(k * BLOCK, BLOCK), BLOCK)
        return pltpu.make_async_remote_copy(
            src_ref=xs.at[rows, :], dst_ref=xr.at[rows, :],
            send_sem=x_send.at[k], recv_sem=x_recv.at[k],
            device_id=partner(me, *steps(k)), device_id_type=MESH,
        )

    def source(k):
        step_y, step_z = steps(k)
        return partner(me, (NY - step_y) % NY, (4 - step_z) % 4)

    def g_copy(k):
        rows = pl.ds(pl.multiple_of(k * BLOCK, BLOCK), BLOCK)
        return pltpu.make_async_remote_copy(
            src_ref=gs.at[rows, :], dst_ref=gr.at[rows, :],
            send_sem=g_send.at[k], recv_sem=g_recv.at[k],
            device_id=source(k), device_id_type=MESH,
        )

    def c_copy(k):
        return pltpu.make_async_remote_copy(
            src_ref=cs.at[k // 8], dst_ref=cr.at[k],
            send_sem=c_send.at[k], recv_sem=c_recv.at[k],
            device_id=source(k), device_id_type=MESH,
        )

    def loop(low, high, act):
        def step(i, carry):
            act(i)
            return carry
        lax.fori_loop(low, high, step, 0)

    loads[1].wait()
    loads[2].wait()

    def dispatch(group):
        rows = pl.ds(pl.multiple_of(group * ROWS, ROWS), ROWS)
        v = vxt[rows, :].astype(jnp.int32)
        row = sub % BLOCK
        put = one((v == row) & (row < CAP))
        parts = (tok[:, :DY_TAIL], tok[:, DY_TAIL:], cot[:, :DY_TAIL])
        for j, part in enumerate(parts):
            put_end = one((v == 3 * (row - CAP) + j) & (row >= CAP))
            got = nn(put, part) + nn(put_end, cot[:, DY_TAIL:])
            xs[rows, j * DY_TAIL : (j + 1) * DY_TAIL] = got.astype(BF16)

    def ring(chunk, act):
        def some(i):
            for q in (1, 2, 3, 0):
                k = chunk * 16 + q * 4 + (i + q) % 4
                if q == 0:
                    pl.when(k > 0)(functools.partial(act, k))
                else:
                    act(k)

        loop(0, 4, some)

    loop(0, 2, dispatch)
    ring(0, lambda k: x_copy(k).start())
    loop(2, 4, dispatch)
    ring(1, lambda k: x_copy(k).start())
    xr[0:BLOCK, :] = xs[0:BLOCK, :]

    up, down, across = [], [], []

    def to_twin(half, step, piece=None):
        twins.append(send_w(shard(half, 0, step, piece), shard(half, 1, step, piece), twin))

    def from_z(p):
        z_in[p].wait_recv()
        up.append(send_w(shard(1, 0, 0, p), shard(1, 0, 1, p), x_up))
        down.append(send_w(shard(1, 0, 0, p), shard(1, 0, 3, p), x_down))
        to_twin(1, 0, p)

    def from_x(p):
        down[p].wait_recv()
        across.append(send_w(shard(1, 0, 3, p), shard(1, 0, 2, p), x_down))
        to_twin(1, 3, p)
        up[p].wait_recv()
        to_twin(1, 1, p)

    def from_across(p):
        across[p].wait_recv()
        to_twin(1, 2, p)

    up0.wait_recv()
    across0 = send_w(shard(0, 0, 1), shard(0, 0, 2), x_up)
    to_twin(0, 1)
    down0.wait_recv()
    to_twin(0, 3)
    from_z(0)
    across0.wait_recv()
    to_twin(0, 2)
    from_z(1)
    from_x(0)
    from_z(2)
    from_x(1)
    from_across(0)
    from_x(2)
    from_across(1)
    from_across(2)
    for copy in twins:
        copy.wait_recv()
    loads[4].wait()

    sub2 = iota((WIDE, WIDE), 0)
    lane2 = iota((WIDE, WIDE), 1)
    row2 = sub2 % BLOCK
    col2 = lane2 % BLOCK
    same2 = sub2 // BLOCK == lane2 // BLOCK

    def work(chunk):
        loop(jnp.where(chunk == 0, 1, 16), 16 + 16 * chunk, lambda k: x_copy(k).wait_recv())
        rows = pl.ds(pl.multiple_of(chunk * WIDE, WIDE), WIDE)
        end = jnp.zeros((WIDE, DY_TAIL), F32)
        for j in range(3):
            take = one(same2 & (col2 >= CAP) & (row2 == 3 * (col2 - CAP) + j))
            end = end + nn(take, xr[rows, j * DY_TAIL : (j + 1) * DY_TAIL])
        tail[...] = end.astype(BF16)

        def units(t, total):
            us = pl.ds(pl.multiple_of(t * TILE, TILE), TILE)
            xv = xr[rows, 0:D]
            gate = nt(xv, wb[us, 0:D])
            up_pre = nt(xv, wb[us, D : 2 * D])
            back = nt(xr[rows, D : D + DY_TAIL], wb[us, 2 * D : 2 * D + DY_TAIL])
            back = back + nt(tail[...], wb[us, 2 * D + DY_TAIL : 3 * D])
            sig = jax.nn.sigmoid(gate)
            act = gate * sig
            d_up = back * act
            d_gate = back * up_pre * (sig * (1.0 + gate * (1.0 - sig)))
            dgs[:, us] = d_gate.astype(BF16)
            dus[:, us] = d_up.astype(BF16)
            return total + jnp.sum(d_up * up_pre, axis=1, keepdims=True)

        total = lax.fori_loop(0, UNITS // TILE, units, jnp.zeros((WIDE, 1), F32))
        for h in range(2):
            part = jnp.broadcast_to(total[h * ROWS : (h + 1) * ROWS, :], (ROWS, ROWS))
            cs[chunk * 2 + h] = jnp.transpose(part)[0:1, :]

        def grad(low):
            high = low + G_TAIL
            return nn(dgs[...], wb[:, low:high]) + nn(dus[...], wb[:, D + low : D + high])

        ends[...] = grad(BACK).astype(BF16)
        for j in range(3):
            take = one(same2 & (row2 >= CAP) & (col2 == 3 * (row2 - CAP) + j))
            moved = nn(take, ends[...])
            keep = iota((WIDE, G_TAIL), 0) % BLOCK < CAP
            both = jnp.where(keep, grad(j * G_TAIL), moved).astype(BF16)
            gs[rows, j * G_TAIL : (j + 1) * G_TAIL] = both

        def give(k):
            g_copy(k).start()
            c_copy(k).start()

        ring(chunk, give)

    loop(0, 2, work)
    gr[0:BLOCK, :] = gs[0:BLOCK, :]
    cr[0] = cs[0]

    loads[3].wait()
    c0, c1 = column(cmb[0:1, :])[:, 0:1], column(cmb[1:2, :])[:, 0:1]
    first, second = first[:, 0:1], second[:, 0:1]
    wide_lane = iota((ROWS, WIDE), 1)
    col = wide_lane % BLOCK

    def arrived(k):
        g_copy(k).wait_recv()
        c_copy(k).wait_recv()

    def gone(k):
        g_copy(k).wait_send()
        c_copy(k).wait_send()

    def gather(chunk, sums):
        rows = slice(chunk * WIDE, (chunk + 1) * WIDE)
        v = vx[:, rows].astype(jnp.int32)
        block = chunk * 16 + wide_lane // BLOCK
        at0, at1 = first == block, second == block
        scale = jnp.where(at0, c0, c1)
        hit = (v == col) & (col < CAP)
        put = jnp.where(hit, scale, 0.0).astype(BF16)
        hit0 = jnp.where(hit & at0, 1.0, 0.0)
        hit1 = jnp.where(hit & at1, 1.0, 0.0)
        loop(max(1, chunk * 16), chunk * 16 + 16, arrived)
        end = jnp.zeros((ROWS, G_TAIL), F32)
        for j in range(3):
            cols = slice(j * G_TAIL, (j + 1) * G_TAIL)
            hit_end = (v == 3 * (col - CAP) + j) & (col >= CAP)
            put_end = jnp.where(hit_end, scale, 0.0).astype(BF16)
            got = nn(jnp.concatenate([put, put_end], axis=0), gr[rows, cols])
            end = end + got[ROWS:, :]
            if chunk == 0:
                home[:, cols] = got[:ROWS, :]
            else:
                out[:, cols] = (home[:, cols] + got[:ROWS, :]).astype(BF16)
        if chunk == 0:
            home[:, BACK:D] = end
        else:
            out[:, BACK:D] = (home[:, BACK:D] + end).astype(BF16)
        g0, g1 = sums
        for h in range(2):
            line = jnp.zeros((1, ROWS), F32)
            for i in range(8):
                mine = iota((1, ROWS), 1) // BLOCK == i
                line = jnp.where(mine, cr[chunk * 16 + h * 8 + i], line)
            part = slice(h * ROWS, (h + 1) * ROWS)
            g0 = g0 + jnp.sum(hit0[:, part] * line, axis=1, keepdims=True)
            g1 = g1 + jnp.sum(hit1[:, part] * line, axis=1, keepdims=True)
        return g0, g1

    loop(1, BLOCKS, lambda k: x_copy(k).wait_send())
    for copy in started:
        copy.wait_send()
    zero = jnp.zeros((ROWS, 1), F32)
    sums = gather(0, (zero, zero))
    loop(1, BLOCKS, gone)
    g0, g1 = gather(1, sums)
    gcomb[0:1, :] = jnp.transpose(jnp.broadcast_to(g0, (ROWS, ROWS)))[0:1, :]
    gcomb[1:2, :] = jnp.transpose(jnp.broadcast_to(g1, (ROWS, ROWS)))[0:1, :]


def body(tokens, cotangent, expert_weights, route_ids, combine):
    vmem = pl.BlockSpec(memory_space=pltpu.VMEM)
    hbm = pl.BlockSpec(memory_space=pltpu.HBM)
    slots = BLOCKS * BLOCK
    dma = pltpu.SemaphoreType.DMA
    grad_tokens, grad_combine = pl.pallas_call(
        kernel,
        out_shape=(
            jax.ShapeDtypeStruct((ROWS, D), BF16),
            jax.ShapeDtypeStruct((2, ROWS), F32),
        ),
        in_specs=[hbm] * 5,
        out_specs=(vmem, vmem),
        scratch_shapes=[
            pltpu.VMEM((ROWS, D), BF16),
            pltpu.VMEM((ROWS, D), BF16),
            pltpu.VMEM((2, ROWS), jnp.int32),
            pltpu.VMEM((2, ROWS), F32),
            pltpu.VMEM((UNITS, 3 * D), BF16),
            pltpu.VMEM((slots, SEND), BF16),
            pltpu.VMEM((slots, SEND), BF16),
            pltpu.VMEM((slots, BACK), BF16),
            pltpu.VMEM((slots, BACK), BF16),
            pltpu.VMEM((WIDE, DY_TAIL), BF16),
            pltpu.VMEM((WIDE, G_TAIL), BF16),
            pltpu.VMEM((WIDE, UNITS), BF16),
            pltpu.VMEM((WIDE, UNITS), BF16),
            pltpu.VMEM((ROWS, D), F32),
            pltpu.VMEM((GROUPS, 1, ROWS), F32),
            pltpu.VMEM((BLOCKS, 1, ROWS), F32),
            pltpu.VMEM((ROWS, slots), F32),
            pltpu.VMEM((slots, ROWS), F32),
            dma((5,)),
            dma((W_COPIES,)), dma((W_COPIES,)),
            dma((BLOCKS,)), dma((BLOCKS,)),
            dma((BLOCKS,)), dma((BLOCKS,)),
            dma((BLOCKS,)), dma((BLOCKS,)),
        ],
        compiler_params=pltpu.CompilerParams(
            collective_id=0, has_side_effects=True, vmem_limit_bytes=56 << 20
        ),
        cost_estimate=pl.CostEstimate(flops=8 << 30, bytes_accessed=4 << 20, transcendentals=1 << 20),
    )(tokens, cotangent, expert_weights[0], route_ids.T, combine.T)
    return grad_tokens, grad_combine.T


def solution(mesh):
    rows = P(("dp", "ctx", "exp"), None)
    return jax.shard_map(
        body,
        mesh=mesh,
        in_specs=(rows, rows, P("exp", ("dp", "ctx"), None), rows, rows),
        out_specs=(rows, rows),
        check_vma=False,
    )
```

```python
import functools

import jax
import jax.numpy as jnp
from jax import lax
from jax.experimental import pallas as pl
from jax.experimental.pallas import tpu as pltpu
from jax.sharding import PartitionSpec as P

MESH = pl.DeviceIdType.MESH
BF16 = jnp.bfloat16
F32 = jnp.float32
ROWS = 128
CAP = 12
BLOCK = 16
BLOCKS = 32
GROUPS = 4
WIDE = 256
NX, NY, NZ = 4, 8, 8
D = 2048
SEND = 3 * D // 2
BACK = 3 * D // 4
DY_TAIL = D // 2
G_TAIL = D // 4
UNITS = 768
SHARD = 48
PIECE = 16
W_COPIES = 31
TILE = 256


def place():
    core = lax.axis_index("dp")
    ctx = lax.axis_index("ctx")
    exp = lax.axis_index("exp")
    return core, ctx % NX, exp % NY, (ctx // NX) * 4 + exp // NY


def device(core, x, y, z):
    return (core, (z // 4) * NX + x, (z % 4) * NY + y)


def partner(me, step_y, step_z):
    core, x, y, z = me
    far = jnp.where(step_z == 2, ((z // 2) % 2 + core) % 2, jnp.where(step_z == 3, 1, 0))
    return device(core, x, (y + step_y) % NY, (z + step_z + 4 * far) % NZ)


def table(index, values):
    found = jnp.full_like(index, values[0])
    for i, value in enumerate(values[1:]):
        found = jnp.where(index == i + 1, value, found)
    return found


def steps(k):
    return table(k // 4, (0, 4, 3, 5, 2, 6, 1, 7)), k % 4


def iota(shape, dim):
    return lax.broadcasted_iota(jnp.int32, shape, dim)


def nt(a, b):
    return lax.dot_general(a, b, (((1,), (1,)), ((), ())), preferred_element_type=F32)


def nn(a, b):
    return jnp.dot(a, b, preferred_element_type=F32)


def one(cond):
    return jnp.where(cond, 1.0, 0.0).astype(BF16)


def kernel(
    tok_hbm, cot_hbm, w_ref, rid_hbm, cmb_hbm, out, gcomb,
    tok, cot, rid, cmb, wb, xs, xr, gs, gr, tail, ends, dgs, dus, home, cs, cr, vx, vxt,
    local_sem, w_send, w_recv, x_send, x_recv, g_send, g_recv, c_send, c_recv,
):
    me = place()
    core, x, y, z = me
    barrier = pltpu.get_barrier_semaphore()

    def greet(k, carry):
        pl.semaphore_signal(
            barrier, inc=1, device_id=partner(me, *steps(k)), device_id_type=MESH
        )
        return carry

    lax.fori_loop(1, BLOCKS, greet, 0)
    z_far = device(core, x, y, (z + 4) % NZ)
    x_up = device(core, (x + 1) % NX, y, z)
    x_down = device(core, (x + 3) % NX, y, z)
    twin = device(1 - core, x, y, z)
    for other in (z_far, x_up, x_down, twin):
        pl.semaphore_signal(barrier, inc=1, device_id=other, device_id_type=MESH)

    def shard(half, side, step, piece=None):
        at = (half * 8 + side * 4 + step) * SHARD
        if piece is None:
            return wb.at[pl.ds(at, SHARD), :]
        return wb.at[pl.ds(at + piece * PIECE, PIECE), :]

    loads = []
    for n, (src, dst) in enumerate(
        ((rid_hbm, rid), (tok_hbm, tok), (cot_hbm, cot), (cmb_hbm, cmb), (w_ref, shard(0, 0, 0)))
    ):
        load = pltpu.make_async_copy(src, dst, local_sem.at[n])
        load.start()
        loads.append(load)
    loads[0].wait()

    ids = rid[...]
    step_z = (ids // NY - z % 4 + 4) % 4
    step_y = (ids % NY - y + NY) % NY
    rel = (table(step_y, (0, 6, 4, 2, 1, 3, 5, 7)) * 4 + step_z).astype(F32)

    def column(line):
        return jnp.transpose(jnp.broadcast_to(line, (ROWS, ROWS)))

    first = column(rel[0:1, :]).astype(jnp.int32)
    second = column(rel[1:2, :]).astype(jnp.int32)
    lane = iota((ROWS, ROWS), 1)
    sub = iota((ROWS, ROWS), 0)
    named = (first == lane) | (second == lane)
    ordinal = nn(one(lane < sub), one(named))
    val = jnp.where(named, ordinal, -1.0).astype(BF16)
    slots = BLOCKS * BLOCK
    spread = one(iota((slots, ROWS), 0) // BLOCK == iota((slots, ROWS), 1))
    vxt[...] = nt(spread, val)
    vx[...] = nt(val, spread)

    pl.semaphore_wait(barrier, BLOCKS - 1 + 4)

    started = []

    def send_w(src, dst, target):
        n = len(started)
        copy = pltpu.make_async_remote_copy(
            src_ref=src, dst_ref=dst, send_sem=w_send.at[n], recv_sem=w_recv.at[n],
            device_id=target, device_id_type=MESH,
        )
        copy.start()
        started.append(copy)
        return copy

    pieces = range(SHARD // PIECE)
    z_in = [
        send_w(w_ref.at[pl.ds(p * PIECE, PIECE), :], shard(1, 0, 0, p), z_far) for p in pieces
    ]
    up0 = send_w(w_ref, shard(0, 0, 1), x_up)
    down0 = send_w(w_ref, shard(0, 0, 3), x_down)
    twins = [send_w(w_ref, shard(0, 1, 0), twin)]

    def x_copy(k):
        rows = pl.ds(pl.multiple_of(k * BLOCK, BLOCK), BLOCK)
        return pltpu.make_async_remote_copy(
            src_ref=xs.at[rows, :], dst_ref=xr.at[rows, :],
            send_sem=x_send.at[k], recv_sem=x_recv.at[k],
            device_id=partner(me, *steps(k)), device_id_type=MESH,
        )

    def source(k):
        step_y, step_z = steps(k)
        return partner(me, (NY - step_y) % NY, (4 - step_z) % 4)

    def g_copy(k):
        rows = pl.ds(pl.multiple_of(k * BLOCK, BLOCK), BLOCK)
        return pltpu.make_async_remote_copy(
            src_ref=gs.at[rows, :], dst_ref=gr.at[rows, :],
            send_sem=g_send.at[k], recv_sem=g_recv.at[k],
            device_id=source(k), device_id_type=MESH,
        )

    def c_copy(k):
        return pltpu.make_async_remote_copy(
            src_ref=cs.at[k // 8], dst_ref=cr.at[k],
            send_sem=c_send.at[k], recv_sem=c_recv.at[k],
            device_id=source(k), device_id_type=MESH,
        )

    def loop(low, high, act):
        def step(i, carry):
            act(i)
            return carry
        lax.fori_loop(low, high, step, 0)

    loads[1].wait()
    loads[2].wait()

    def dispatch(group):
        rows = pl.ds(pl.multiple_of(group * ROWS, ROWS), ROWS)
        v = vxt[rows, :].astype(jnp.int32)
        row = sub % BLOCK
        put = one((v == row) & (row < CAP))
        parts = (tok[:, :DY_TAIL], tok[:, DY_TAIL:], cot[:, :DY_TAIL])
        for j, part in enumerate(parts):
            put_end = one((v == 3 * (row - CAP) + j) & (row >= CAP))
            got = nn(put, part) + nn(put_end, cot[:, DY_TAIL:])
            xs[rows, j * DY_TAIL : (j + 1) * DY_TAIL] = got.astype(BF16)

    def ring(chunk, act):
        def some(i):
            for q in (2, 3, 1, 0):
                k = chunk * 16 + q * 4 + (i + q) % 4
                if q == 0:
                    pl.when(k > 0)(functools.partial(act, k))
                else:
                    act(k)

        loop(0, 4, some)

    loop(0, 2, dispatch)
    ring(0, lambda k: x_copy(k).start())
    loop(2, 4, dispatch)
    ring(1, lambda k: x_copy(k).start())
    xr[0:BLOCK, :] = xs[0:BLOCK, :]

    up, down, across = [], [], []

    def to_twin(half, step, piece=None):
        twins.append(send_w(shard(half, 0, step, piece), shard(half, 1, step, piece), twin))

    def from_z(p):
        z_in[p].wait_recv()
        up.append(send_w(shard(1, 0, 0, p), shard(1, 0, 1, p), x_up))
        down.append(send_w(shard(1, 0, 0, p), shard(1, 0, 3, p), x_down))
        to_twin(1, 0, p)

    def from_x(p):
        down[p].wait_recv()
        across.append(send_w(shard(1, 0, 3, p), shard(1, 0, 2, p), x_down))
        to_twin(1, 3, p)
        up[p].wait_recv()
        to_twin(1, 1, p)

    def from_across(p):
        across[p].wait_recv()
        to_twin(1, 2, p)

    up0.wait_recv()
    across0 = send_w(shard(0, 0, 1), shard(0, 0, 2), x_up)
    to_twin(0, 1)
    down0.wait_recv()
    to_twin(0, 3)
    from_z(0)
    across0.wait_recv()
    to_twin(0, 2)
    from_z(1)
    from_x(0)
    from_z(2)
    from_x(1)
    from_across(0)
    from_x(2)
    from_across(1)
    from_across(2)
    for copy in twins:
        copy.wait_recv()
    loads[4].wait()

    sub2 = iota((WIDE, WIDE), 0)
    lane2 = iota((WIDE, WIDE), 1)
    row2 = sub2 % BLOCK
    col2 = lane2 % BLOCK
    same2 = sub2 // BLOCK == lane2 // BLOCK

    def work(chunk):
        loop(jnp.where(chunk == 0, 1, 16), 16 + 16 * chunk, lambda k: x_copy(k).wait_recv())
        rows = pl.ds(pl.multiple_of(chunk * WIDE, WIDE), WIDE)
        end = jnp.zeros((WIDE, DY_TAIL), F32)
        for j in range(3):
            take = one(same2 & (col2 >= CAP) & (row2 == 3 * (col2 - CAP) + j))
            end = end + nn(take, xr[rows, j * DY_TAIL : (j + 1) * DY_TAIL])
        tail[...] = end.astype(BF16)

        def units(t, total):
            us = pl.ds(pl.multiple_of(t * TILE, TILE), TILE)
            xv = xr[rows, 0:D]
            gate = nt(xv, wb[us, 0:D])
            up_pre = nt(xv, wb[us, D : 2 * D])
            back = nt(xr[rows, D : D + DY_TAIL], wb[us, 2 * D : 2 * D + DY_TAIL])
            back = back + nt(tail[...], wb[us, 2 * D + DY_TAIL : 3 * D])
            sig = jax.nn.sigmoid(gate)
            act = gate * sig
            d_up = back * act
            d_gate = back * up_pre * (sig * (1.0 + gate * (1.0 - sig)))
            dgs[:, us] = d_gate.astype(BF16)
            dus[:, us] = d_up.astype(BF16)
            return total + jnp.sum(d_up * up_pre, axis=1, keepdims=True)

        total = lax.fori_loop(0, UNITS // TILE, units, jnp.zeros((WIDE, 1), F32))
        for h in range(2):
            part = jnp.broadcast_to(total[h * ROWS : (h + 1) * ROWS, :], (ROWS, ROWS))
            cs[chunk * 2 + h] = jnp.transpose(part)[0:1, :]

        def grad(low):
            high = low + G_TAIL
            return nn(dgs[...], wb[:, low:high]) + nn(dus[...], wb[:, D + low : D + high])

        ends[...] = grad(BACK).astype(BF16)
        for j in range(3):
            take = one(same2 & (row2 >= CAP) & (col2 == 3 * (row2 - CAP) + j))
            moved = nn(take, ends[...])
            keep = iota((WIDE, G_TAIL), 0) % BLOCK < CAP
            both = jnp.where(keep, grad(j * G_TAIL), moved).astype(BF16)
            gs[rows, j * G_TAIL : (j + 1) * G_TAIL] = both

        def give(k):
            g_copy(k).start()
            c_copy(k).start()

        ring(chunk, give)

    loop(0, 2, work)
    gr[0:BLOCK, :] = gs[0:BLOCK, :]
    cr[0] = cs[0]

    loads[3].wait()
    c0, c1 = column(cmb[0:1, :])[:, 0:1], column(cmb[1:2, :])[:, 0:1]
    first, second = first[:, 0:1], second[:, 0:1]
    wide_lane = iota((ROWS, WIDE), 1)
    col = wide_lane % BLOCK

    def arrived(k):
        g_copy(k).wait_recv()
        c_copy(k).wait_recv()

    def gone(k):
        g_copy(k).wait_send()
        c_copy(k).wait_send()

    def gather(chunk, sums):
        rows = slice(chunk * WIDE, (chunk + 1) * WIDE)
        v = vx[:, rows].astype(jnp.int32)
        block = chunk * 16 + wide_lane // BLOCK
        at0, at1 = first == block, second == block
        scale = jnp.where(at0, c0, c1)
        hit = (v == col) & (col < CAP)
        put = jnp.where(hit, scale, 0.0).astype(BF16)
        hit0 = jnp.where(hit & at0, 1.0, 0.0)
        hit1 = jnp.where(hit & at1, 1.0, 0.0)
        loop(max(1, chunk * 16), chunk * 16 + 16, arrived)
        end = jnp.zeros((ROWS, G_TAIL), F32)
        for j in range(3):
            cols = slice(j * G_TAIL, (j + 1) * G_TAIL)
            hit_end = (v == 3 * (col - CAP) + j) & (col >= CAP)
            put_end = jnp.where(hit_end, scale, 0.0).astype(BF16)
            got = nn(jnp.concatenate([put, put_end], axis=0), gr[rows, cols])
            end = end + got[ROWS:, :]
            if chunk == 0:
                home[:, cols] = got[:ROWS, :]
            else:
                out[:, cols] = (home[:, cols] + got[:ROWS, :]).astype(BF16)
        if chunk == 0:
            home[:, BACK:D] = end
        else:
            out[:, BACK:D] = (home[:, BACK:D] + end).astype(BF16)
        g0, g1 = sums
        for h in range(2):
            line = jnp.zeros((1, ROWS), F32)
            for i in range(8):
                mine = iota((1, ROWS), 1) // BLOCK == i
                line = jnp.where(mine, cr[chunk * 16 + h * 8 + i], line)
            part = slice(h * ROWS, (h + 1) * ROWS)
            g0 = g0 + jnp.sum(hit0[:, part] * line, axis=1, keepdims=True)
            g1 = g1 + jnp.sum(hit1[:, part] * line, axis=1, keepdims=True)
        return g0, g1

    loop(1, BLOCKS, lambda k: x_copy(k).wait_send())
    for copy in started:
        copy.wait_send()
    zero = jnp.zeros((ROWS, 1), F32)
    sums = gather(0, (zero, zero))
    loop(1, BLOCKS, gone)
    g0, g1 = gather(1, sums)
    gcomb[0:1, :] = jnp.transpose(jnp.broadcast_to(g0, (ROWS, ROWS)))[0:1, :]
    gcomb[1:2, :] = jnp.transpose(jnp.broadcast_to(g1, (ROWS, ROWS)))[0:1, :]


def body(tokens, cotangent, expert_weights, route_ids, combine):
    vmem = pl.BlockSpec(memory_space=pltpu.VMEM)
    hbm = pl.BlockSpec(memory_space=pltpu.HBM)
    slots = BLOCKS * BLOCK
    dma = pltpu.SemaphoreType.DMA
    grad_tokens, grad_combine = pl.pallas_call(
        kernel,
        out_shape=(
            jax.ShapeDtypeStruct((ROWS, D), BF16),
            jax.ShapeDtypeStruct((2, ROWS), F32),
        ),
        in_specs=[hbm] * 5,
        out_specs=(vmem, vmem),
        scratch_shapes=[
            pltpu.VMEM((ROWS, D), BF16),
            pltpu.VMEM((ROWS, D), BF16),
            pltpu.VMEM((2, ROWS), jnp.int32),
            pltpu.VMEM((2, ROWS), F32),
            pltpu.VMEM((UNITS, 3 * D), BF16),
            pltpu.VMEM((slots, SEND), BF16),
            pltpu.VMEM((slots, SEND), BF16),
            pltpu.VMEM((slots, BACK), BF16),
            pltpu.VMEM((slots, BACK), BF16),
            pltpu.VMEM((WIDE, DY_TAIL), BF16),
            pltpu.VMEM((WIDE, G_TAIL), BF16),
            pltpu.VMEM((WIDE, UNITS), BF16),
            pltpu.VMEM((WIDE, UNITS), BF16),
            pltpu.VMEM((ROWS, D), F32),
            pltpu.VMEM((GROUPS, 1, ROWS), F32),
            pltpu.VMEM((BLOCKS, 1, ROWS), F32),
            pltpu.VMEM((ROWS, slots), F32),
            pltpu.VMEM((slots, ROWS), F32),
            dma((5,)),
            dma((W_COPIES,)), dma((W_COPIES,)),
            dma((BLOCKS,)), dma((BLOCKS,)),
            dma((BLOCKS,)), dma((BLOCKS,)),
            dma((BLOCKS,)), dma((BLOCKS,)),
        ],
        compiler_params=pltpu.CompilerParams(
            collective_id=0, has_side_effects=True, vmem_limit_bytes=56 << 20
        ),
        cost_estimate=pl.CostEstimate(flops=8 << 30, bytes_accessed=4 << 20, transcendentals=1 << 20),
    )(tokens, cotangent, expert_weights[0], route_ids.T, combine.T)
    return grad_tokens, grad_combine.T


def solution(mesh):
    rows = P(("dp", "ctx", "exp"), None)
    return jax.shard_map(
        body,
        mesh=mesh,
        in_specs=(rows, rows, P("exp", ("dp", "ctx"), None), rows, rows),
        out_specs=(rows, rows),
        check_vma=False,
    )
```
